256 devices in a mesh: row: 8 (over z_lo, x), col: 32 (over z_hi, y, core).
Axes of the slice: x: 4, y: 4, z: 8 (z_hi: 4, z_lo: 2; z = z_hi * 2 + z_lo), core: 2. Of those that a mesh axis runs over, the one named last changes fastest.
Arguments:
- hessian_old: float32 [8192, 24576], P('row', 'col'), may hold values from -6 to 6
- gate_rows: bfloat16 [4096, 8192], P('col', 'row'), may hold values from -9 to 9
- up_rows: bfloat16 [4096, 8192], P('col', 'row'), may hold values from -15 to 15
- gate_columns: bfloat16 [4096, 24576], P('row', 'col'), may hold values from -9 to 9
- up_columns: bfloat16 [4096, 24576], P('row', 'col'), may hold values from -15 to 15
Outputs:
- hessian_new: float32 [8192, 24576], P('row', 'col')
The draws below stay inside these ranges and needn't reach their ends.
All inputs are finite; a program needn't handle non-finite values.
Results may differ from the reference program's by a relative error of at most 0.00099.
Values may be sent and summed in bfloat16 or wider, within the bound.
No kernel may reach another device: no remote copies, remote signals or barrier semaphores. Data moves between devices by JAX's collectives and lax.ppermute only.
A program may use at most 64 MiB of HBM per device.

```python
import jax
import jax.numpy as jnp
from jax import lax

TOKENS = 4096
ROWS = 8192
COLS = 24576


def block_scale(key, shape, split, low, high):
    def one(axis_at, shards_of):
        heights = jax.random.uniform(jax.random.fold_in(jax.random.fold_in(key, 6), axis_at), (shards_of,), jnp.float32, low / len(split), high / len(split))
        return jnp.repeat(jnp.exp(heights), shape[axis_at] // shards_of).reshape((-1,) + (1,) * (len(shape) - axis_at - 1))

    level = one(*split[0])
    for cut in split[1:]:
        level = level * one(*cut)
    return level


def gaussian(key, shape, spread, bound, split=(), held_as=jnp.bfloat16):
    loudness = block_scale(key, shape, split, -0.22, 0.18) if split else 1.0
    array = jax.random.normal(key, shape, jnp.float32) * spread * loudness
    return jnp.minimum(jnp.maximum(array, -bound), bound).astype(held_as)


def setup_inputs(seed: int = 0) -> dict:
    splits = jax.random.split(jax.random.key(seed), 6)
    hessian_old = gaussian(splits[0], (ROWS, COLS), 1.0, 6.0, ((0, 8), (1, 32)), jnp.float32)
    gate_rows = gaussian(splits[1], (TOKENS, ROWS), 1.5, 9.0, ((0, 32), (1, 8)))
    up_rows = gaussian(splits[2], (TOKENS, ROWS), 2.5, 15.0, ((0, 32), (1, 8)))
    gate_columns = gaussian(splits[3], (TOKENS, COLS), 1.5, 9.0, ((0, 8), (1, 32)))
    up_columns = gaussian(splits[4], (TOKENS, COLS), 2.5, 15.0, ((0, 8), (1, 32)))
    return dict(hessian_old=hessian_old, gate_rows=gate_rows, up_rows=up_rows, gate_columns=gate_columns, up_columns=up_columns)


def silu_product(gate, up):
    return (jax.nn.silu(gate.astype(jnp.float32)) * up.astype(jnp.float32)).astype(jnp.bfloat16)


def reference(hessian_old, gate_rows, up_rows, gate_columns, up_columns):
    row_inputs = silu_product(gate_rows, up_rows)
    column_inputs = silu_product(gate_columns, up_columns)
    product = lax.dot_general(row_inputs, column_inputs, (((0,), (0,)), ((), ())), preferred_element_type=jnp.float32)
    return 0.5 * hessian_old + product / TOKENS
```

```python
import jax
import jax.numpy as jnp
from jax import lax
from jax.sharding import PartitionSpec as P

AXES = ("row", "col")


def place(x, y, z, c):
    x, y, z = x % 4, y % 4, z % 8
    return ((z % 2) * 4 + x) * 32 + ((z // 2) * 4 + y) * 2 + c


def send(value, dx=0, dy=0, dz=0, swap_z=False, swap_core=False):
    pairs = []
    for x in range(4):
        for y in range(4):
            for z in range(8):
                for c in range(2):
                    to_z = (z ^ 1) if swap_z else z + dz
                    pairs.append((place(x, y, z, c), place(x + dx, y + dy, to_z, c ^ int(swap_core))))
    return lax.ppermute(value, AXES, pairs)


def silu_product(gate, up):
    return (jax.nn.silu(gate.astype(jnp.float32)) * up.astype(jnp.float32)).astype(jnp.bfloat16)


def body(hessian_old, gate_rows, up_rows, gate_columns, up_columns):
    total_tokens = lax.axis_size("col") * gate_rows.shape[0]
    row, col = lax.axis_index("row"), lax.axis_index("col")
    zl, x = row // 4, row % 4
    zh, y, c = col // 8, (col // 2) % 4, col % 2

    own = silu_product(gate_columns, up_columns)
    own_rows = silu_product(gate_rows, up_rows)

    pair = send(own, swap_z=True)
    columns = {(0, 0): own, (1, 0): pair}
    columns[0, 2] = send(own, dx=2)
    z_rows = {0: own_rows, 2: send(own_rows, dz=4), 1: send(own_rows, dz=2), 3: send(own_rows, dz=-2)}
    columns[0, 1] = send(own, dx=1)
    columns[0, 3] = send(own, dx=-1)
    columns[1, 2] = send(pair, dx=2)
    columns[1, 1] = send(pair, dx=1)
    columns[1, 3] = send(pair, dx=-1)

    z_block = jnp.zeros((4,) + own_rows.shape, own_rows.dtype)
    for back, block in z_rows.items():
        z_block = lax.dynamic_update_slice(z_block, block[None], ((zh - back) % 4, 0, 0))
    y_blocks = {0: z_block, 2: send(z_block, dy=2), 1: send(z_block, dy=1), 3: send(z_block, dy=-1)}
    rows = jnp.zeros((4, 4, 2) + own_rows.shape, own_rows.dtype)
    for back, block in y_blocks.items():
        rows = lax.dynamic_update_slice(rows, block[:, None, None], (0, (y - back) % 4, c, 0, 0))
        other = send(block, swap_core=True)
        rows = lax.dynamic_update_slice(rows, other[:, None, None], (0, (y - back) % 4, 1 - c, 0, 0))
    rows = rows.reshape(4096, -1)

    total = 0.5 * hessian_old
    for (back_z, back_x), block in columns.items():
        shard = ((zl + back_z) % 2) * 4 + (x - back_x) % 4
        part = lax.dynamic_slice(rows, (shard * 512, 0), (512, rows.shape[1]))
        product = lax.dot_general(part, block, (((0,), (0,)), ((), ())), preferred_element_type=jnp.float32)
        total = total + product / total_tokens
    return total


def solution(mesh):
    in_specs = (P("row", "col"), P("col", "row"), P("col", "row"), P("row", "col"), P("row", "col"))
    out_specs = P("row", "col")
    return jax.shard_map(body, mesh=mesh, in_specs=in_specs, out_specs=out_specs, check_vma=False)
```

```python
import functools

import jax
import jax.numpy as jnp
from jax import lax
from jax.experimental import pallas as pl
from jax.experimental.pallas import tpu as pltpu
from jax.sharding import PartitionSpec as P

AXES = ("row", "col")
CHUNK = 512
VMEM = pl.BlockSpec(memory_space=pltpu.VMEM)
SMEM = pl.BlockSpec(memory_space=pltpu.SMEM)
HBM = pl.BlockSpec(memory_space=pltpu.HBM)


def place(x, y, z, c):
    x, y, z = x % 4, y % 4, z % 8
    return ((z % 2) * 4 + x) * 32 + ((z // 2) * 4 + y) * 2 + c


def send(value, target, after=()):
    if after:
        value = lax.optimization_barrier((value, *after))[0]
    pairs = []
    for x in range(4):
        for y in range(4):
            for z in range(8):
                for c in range(2):
                    pairs.append((place(x, y, z, c), place(*target(x, y, z, c))))
    return lax.ppermute(value, AXES, pairs)


def way(c):
    return 1 - 2 * c


def x_out(x, y, z, c):
    return x + way(c), y, z, c


def x_back(x, y, z, c):
    return x - way(c), y, z, c


def y_out(x, y, z, c):
    return x, y + way(c), z, c


def y_back(x, y, z, c):
    return x, y - way(c), z, c


def z_out(x, y, z, c):
    return x, y, z + 2 * way(c), c


def z_back(x, y, z, c):
    return x, y, z - 2 * way(c), c


def z_swap(x, y, z, c):
    return x, y, z ^ 1, c


def core_swap(x, y, z, c):
    return x, y, z, 1 - c


MOVES = {x_out: (1, 0, 0), x_back: (-1, 0, 0), y_out: (1, 0, 0), y_back: (-1, 0, 0), z_out: (0, 1, 0), z_back: (0, -1, 0), z_swap: (0, 1, 0), core_swap: (0, 0, 1)}


def silu_product(gate, up):
    return (jax.nn.silu(gate.astype(jnp.float32)) * up.astype(jnp.float32)).astype(jnp.bfloat16)


def rows_kernel(gate, up, out):
    gated = gate[...].astype(jnp.float32)
    formed = gated / (1.0 + jnp.exp(-gated)) * up[...].astype(jnp.float32)
    out[0] = formed.T.astype(jnp.bfloat16)


def form_rows(gate, up):
    tokens, units = gate.shape
    return pl.pallas_call(
        rows_kernel,
        out_shape=jax.ShapeDtypeStruct((1, units, tokens), jnp.bfloat16),
        in_specs=[VMEM, VMEM],
        out_specs=VMEM,
        cost_estimate=pl.CostEstimate(flops=8 * gate.size, bytes_accessed=6 * gate.size, transcendentals=gate.size),
    )(gate, up)


def add_up(n, ready, left, cols, acc, first, first_ready, first_scale, scale, out, out_sems):
    units = acc.shape[0]
    done = []
    for index in range(n):
        ready(index)
        for step in range(units // CHUNK):
            part = pl.ds(step * CHUNK, CHUNK)
            product = jnp.dot(left(index, part), cols[index], preferred_element_type=jnp.float32)
            if index == 0:
                acc[part, :] = product
            elif index < n - 1:
                acc[part, :] += product
            else:
                if step == 0:
                    first_ready()
                acc[part, :] = first_scale * first[part, :] + scale * (acc[part, :] + product)
                done.append(pltpu.make_async_copy(acc.at[part], out.at[part], out_sems.at[step]))
                done[-1].start()
    for copy in done:
        copy.wait()


def early_kernel(n_pieces, n_columns, scale, table, hessian, *refs):
    pieces, columns = refs[:n_pieces], refs[n_pieces:n_pieces + n_columns]
    out, late_rows, rows, cols, old, acc, row_sems, col_sems, old_sem, late_sems, out_sems = refs[n_pieces + n_columns:]
    n_blocks = rows.shape[0]
    shard_at = lambda i: table[n_blocks + i]
    col_copies = [pltpu.make_async_copy(block, cols.at[i], col_sems.at[i]) for i, block in enumerate(columns)]
    old_copy = pltpu.make_async_copy(hessian, old, old_sem)
    col_copies[0].start()
    k = 0
    for piece in pieces:
        for i in range(piece.shape[0]):
            at = table[k]
            pltpu.make_async_copy(piece.at[i], rows.at[at], row_sems.at[at]).start()
            k += 1
    for copy in col_copies[1:]:
        copy.start()
    old_copy.start()
    kept = []

    def rows_ready(index):
        for i in range(4):
            at = shard_at(index) * 4 + i
            pltpu.make_async_copy(rows.at[at], rows.at[at], row_sems.at[at]).wait()

    def ready(index):
        rows_ready(index)
        col_copies[index].wait()

    def old_ready():
        old_copy.wait()
        for j in range(late_rows.shape[0] // 4):
            rows_ready(n_columns + j)
            for i in range(4):
                at = shard_at(n_columns + j) * 4 + i
                kept.append(pltpu.make_async_copy(rows.at[at], late_rows.at[j * 4 + i], late_sems.at[j * 4 + i]))
                kept[-1].start()

    def left(index, part):
        at = shard_at(index) * 4
        return jnp.concatenate([rows[at + i, part, :] for i in range(4)], axis=1)

    add_up(n_columns, ready, left, cols, acc, old, old_ready, 0.5, scale, out, out_sems)
    for copy in kept:
        copy.wait()


def late_kernel(n_columns, scale, partial, late_rows, *refs):
    columns = refs[:n_columns]
    out, rows, cols, old, acc, row_sems, col_sems, old_sem, out_sems = refs[n_columns:]
    row_copies, col_copies = [], []
    for i, block in enumerate(columns):
        own = pl.ds(i * 4, 4)
        row_copies.append(pltpu.make_async_copy(late_rows.at[own], rows.at[own], row_sems.at[i]))
        col_copies.append(pltpu.make_async_copy(block, cols.at[i], col_sems.at[i]))
        row_copies[-1].start()
        col_copies[-1].start()
    old_copy = pltpu.make_async_copy(partial, old, old_sem)
    old_copy.start()

    def ready(index):
        row_copies[index].wait()
        col_copies[index].wait()

    def left(index, part):
        return jnp.concatenate([rows[index * 4 + i, part, :] for i in range(4)], axis=1)

    add_up(n_columns, ready, left, cols, acc, old, old_copy.wait, 1.0, scale, out, out_sems)


def cost(columns, units):
    k = sum(b.shape[0] for b in columns)
    wide = columns[0].shape[1]
    return pl.CostEstimate(flops=2 * k * units * wide, bytes_accessed=8 * units * wide + 2 * k * (units + wide), transcendentals=0)


def body(hessian_old, gate_rows, up_rows, gate_columns, up_columns):
    tokens = lax.axis_size("col") * gate_rows.shape[0]
    row, col = lax.axis_index("row"), lax.axis_index("col")
    zl, x = row // 4, row % 4
    zh, y, c = col // 8, (col // 2) % 4, col % 2
    w = way(c)
    cat = lambda *blocks: jnp.concatenate(blocks, axis=0)

    r0 = form_rows(gate_rows, up_rows)
    own = silu_product(gate_columns, up_columns)

    plan = (
        ("za", ("r0",), z_out),
        ("ya1", ("r0",), y_out),
        ("yb1", ("r0",), y_back),
        ("zb", ("r0",), z_back),
        ("xb", ("own",), x_back),
        ("za",),
        ("zf", ("za",), z_out),
        ("ya1",),
        ("yf1", ("ya1",), y_out),
        ("yb1",),
        ("xa", ("own",), x_out),
        ("zb",),
        ("pair", ("own",), z_swap),
        ("xb",),
        ("ya2", ("za", "zb", "zf",), y_out),
        ("zf",),
        ("k1", ("ya1", "yb1", "yf1",), core_swap),
        ("yf1",),
        ("xf", ("xa",), x_out),
        ("xa",),
        ("yb2", ("za", "zb", "zf",), y_back),
        ("pair",),
        ("yf2", ("ya2",), y_out),
        ("ya2",),
        ("xb2", ("pair",), x_back),
        ("k1",),
        ("xf2", ("xf",), z_swap),
        ("xf",),
        ("k0", ("r0", "za", "zb", "zf",), core_swap),
        ("yb2",),
        ("xa2", ("pair",), x_out),
        ("yf2",),
        ("k2", ("ya2", "yb2", "yf2",), core_swap),
        ("k0",),
        ("k2",),
    )
    got = {"r0": r0, "own": own}
    came = {"r0": [(0, 0, 0)], "own": [(0, 0, 0)]}
    for name, *way_there in plan:
        if way_there:
            sources, target = way_there
            move = MOVES[target]
            came[name] = [tuple(p + q for p, q in zip(at, move)) for k in sources for at in came[k]]
    early_names, late_names = ("own", "pair", "xa", "xb", "xf",), ("xa2", "xb2", "xf2",)
    piece_names = ["r0"] + [name for name in came if name[0] in "zyk"]

    def token_block(side, up, other):
        sign = w * (1 - 2 * other)
        return ((zh - sign * up) % 4) * 8 + ((y - sign * side) % 4) * 2 + (c + other) % 2

    def shard(side, up, other):
        return ((zl + up) % 2) * 4 + (x - w * side) % 4

    block_at = [token_block(*at) for name in piece_names for at in came[name]]
    shard_at = [shard(*came[name][0]) for name in early_names + late_names]
    table = jnp.stack(block_at + shard_at).astype(jnp.int32) - 16
    for name, *way_there in plan:
        if way_there:
            sources, target = way_there
            value = got[sources[0]] if len(sources) == 1 else cat(*(got[k] for k in sources))
            table, value = lax.optimization_barrier((table, value))
            got[name] = send(value, target)
        else:
            table, got[name] = lax.optimization_barrier((table + 1, got[name]))

    pieces = [got[name] for name in piece_names]
    early = [got[name] for name in early_names]
    late = [got[name] for name in late_names]
    units, wide = hessian_old.shape
    scale = 1.0 / tokens
    n_blocks = tokens // 128
    n_late = 4 * len(late)
    params = pltpu.CompilerParams(vmem_limit_bytes=58 * 2**20)
    whole = pltpu.VMEM(hessian_old.shape, jnp.float32)
    dma = pltpu.SemaphoreType.DMA
    partial, late_rows = pl.pallas_call(
        functools.partial(early_kernel, len(pieces), len(early), scale),
        out_shape=(jax.ShapeDtypeStruct(hessian_old.shape, jnp.float32), jax.ShapeDtypeStruct((n_late, units, 128), jnp.bfloat16)),
        in_specs=[SMEM, HBM] + [HBM] * (len(pieces) + len(early)),
        out_specs=(HBM, HBM),
        scratch_shapes=[
            pltpu.VMEM((n_blocks, units, 128), jnp.bfloat16),
            pltpu.VMEM((len(early), *own.shape), jnp.bfloat16),
            whole,
            whole,
            dma((n_blocks,)),
            dma((len(early),)),
            dma,
            dma((n_late,)),
            dma((units // CHUNK,)),
        ],
        compiler_params=params,
        cost_estimate=cost(early, units),
    )(table, hessian_old, *pieces, *early)
    partial, *late = lax.optimization_barrier((partial, *late))
    return pl.pallas_call(
        functools.partial(late_kernel, len(late), scale),
        out_shape=jax.ShapeDtypeStruct(hessian_old.shape, jnp.float32),
        in_specs=[HBM] * (2 + len(late)),
        out_specs=HBM,
        scratch_shapes=[
            pltpu.VMEM((n_late, units, 128), jnp.bfloat16),
            pltpu.VMEM((len(late), *own.shape), jnp.bfloat16),
            whole,
            whole,
            dma((len(late),)),
            dma((len(late),)),
            dma,
            dma((units // CHUNK,)),
        ],
        compiler_params=params,
        cost_estimate=cost(late, units),
    )(partial, late_rows, *late)


def solution(mesh):
    in_specs = (P("row", "col"), P("col", "row"), P("col", "row"), P("row", "col"), P("row", "col"))
    out_specs = P("row", "col")
    return jax.shard_map(body, mesh=mesh, in_specs=in_specs, out_specs=out_specs, check_vma=False)
```

```python
import functools

import jax
import jax.numpy as jnp
from jax import lax
from jax.experimental import pallas as pl
from jax.experimental.pallas import tpu as pltpu
from jax.sharding import PartitionSpec as P

AXES = ("row", "col")
CHUNK = 512
VMEM = pl.BlockSpec(memory_space=pltpu.VMEM)
SMEM = pl.BlockSpec(memory_space=pltpu.SMEM)
HBM = pl.BlockSpec(memory_space=pltpu.HBM)


def place(x, y, z, c):
    x, y, z = x % 4, y % 4, z % 8
    return ((z % 2) * 4 + x) * 32 + ((z // 2) * 4 + y) * 2 + c


def send(value, target, after=()):
    if after:
        value = lax.optimization_barrier((value, *after))[0]
    pairs = []
    for x in range(4):
        for y in range(4):
            for z in range(8):
                for c in range(2):
                    pairs.append((place(x, y, z, c), place(*target(x, y, z, c))))
    return lax.ppermute(value, AXES, pairs)


def way(c):
    return 1 - 2 * c


def x_out(x, y, z, c):
    return x + way(c), y, z, c


def x_back(x, y, z, c):
    return x - way(c), y, z, c


def y_out(x, y, z, c):
    return x, y + way(c), z, c


def y_back(x, y, z, c):
    return x, y - way(c), z, c


def z_out(x, y, z, c):
    return x, y, z + 2 * way(c), c


def z_back(x, y, z, c):
    return x, y, z - 2 * way(c), c


def z_swap(x, y, z, c):
    return x, y, z ^ 1, c


def core_swap(x, y, z, c):
    return x, y, z, 1 - c


MOVES = {x_out: (1, 0, 0), x_back: (-1, 0, 0), y_out: (1, 0, 0), y_back: (-1, 0, 0), z_out: (0, 1, 0), z_back: (0, -1, 0), z_swap: (0, 1, 0), core_swap: (0, 0, 1)}


def silu_product(gate, up):
    return (jax.nn.silu(gate.astype(jnp.float32)) * up.astype(jnp.float32)).astype(jnp.bfloat16)


def rows_kernel(gate, up, out):
    gated = gate[...].astype(jnp.float32)
    formed = gated / (1.0 + jnp.exp(-gated)) * up[...].astype(jnp.float32)
    out[0] = formed.T.astype(jnp.bfloat16)


def form_rows(gate, up):
    tokens, units = gate.shape
    return pl.pallas_call(
        rows_kernel,
        out_shape=jax.ShapeDtypeStruct((1, units, tokens), jnp.bfloat16),
        in_specs=[VMEM, VMEM],
        out_specs=VMEM,
        cost_estimate=pl.CostEstimate(flops=8 * gate.size, bytes_accessed=6 * gate.size, transcendentals=gate.size),
    )(gate, up)


def add_up(n, ready, left, cols, acc, first, first_ready, first_scale, scale, out, out_sems):
    units = acc.shape[0]
    done = []
    for index in range(n):
        ready(index)
        for step in range(units // CHUNK):
            part = pl.ds(step * CHUNK, CHUNK)
            product = jnp.dot(left(index, part), cols[index], preferred_element_type=jnp.float32)
            if index == 0:
                acc[part, :] = product
            elif index < n - 1:
                acc[part, :] += product
            else:
                if step == 0:
                    first_ready()
                acc[part, :] = first_scale * first[part, :] + scale * (acc[part, :] + product)
                done.append(pltpu.make_async_copy(acc.at[part], out.at[part], out_sems.at[step]))
                done[-1].start()
    for copy in done:
        copy.wait()


def early_kernel(n_pieces, n_columns, scale, table, hessian, *refs):
    pieces, columns = refs[:n_pieces], refs[n_pieces:n_pieces + n_columns]
    out, late_rows, rows, cols, old, acc, row_sems, col_sems, old_sem, late_sems, out_sems = refs[n_pieces + n_columns:]
    n_blocks = rows.shape[0]
    shard_at = lambda i: table[n_blocks + i]
    col_copies = [pltpu.make_async_copy(block, cols.at[i], col_sems.at[i]) for i, block in enumerate(columns)]
    old_copy = pltpu.make_async_copy(hessian, old, old_sem)
    col_copies[0].start()
    k = 0
    for piece in pieces:
        for i in range(piece.shape[0]):
            at = table[k]
            pltpu.make_async_copy(piece.at[i], rows.at[at], row_sems.at[at]).start()
            k += 1
    for copy in col_copies[1:]:
        copy.start()
    old_copy.start()
    kept = []

    def rows_ready(index):
        for i in range(4):
            at = shard_at(index) * 4 + i
            pltpu.make_async_copy(rows.at[at], rows.at[at], row_sems.at[at]).wait()

    def ready(index):
        rows_ready(index)
        col_copies[index].wait()

    def old_ready():
        old_copy.wait()
        for j in range(late_rows.shape[0] // 4):
            rows_ready(n_columns + j)
            for i in range(4):
                at = shard_at(n_columns + j) * 4 + i
                kept.append(pltpu.make_async_copy(rows.at[at], late_rows.at[j * 4 + i], late_sems.at[j * 4 + i]))
                kept[-1].start()

    def left(index, part):
        at = shard_at(index) * 4
        return jnp.concatenate([rows[at + i, part, :] for i in range(4)], axis=1)

    add_up(n_columns, ready, left, cols, acc, old, old_ready, 0.5, scale, out, out_sems)
    for copy in kept:
        copy.wait()


def late_kernel(n_columns, scale, partial, late_rows, *refs):
    columns = refs[:n_columns]
    out, rows, cols, old, acc, row_sems, col_sems, old_sem, out_sems = refs[n_columns:]
    row_copies, col_copies = [], []
    for i, block in enumerate(columns):
        own = pl.ds(i * 4, 4)
        row_copies.append(pltpu.make_async_copy(late_rows.at[own], rows.at[own], row_sems.at[i]))
        col_copies.append(pltpu.make_async_copy(block, cols.at[i], col_sems.at[i]))
        row_copies[-1].start()
        col_copies[-1].start()
    old_copy = pltpu.make_async_copy(partial, old, old_sem)
    old_copy.start()

    def ready(index):
        row_copies[index].wait()
        col_copies[index].wait()

    def left(index, part):
        return jnp.concatenate([rows[index * 4 + i, part, :] for i in range(4)], axis=1)

    add_up(n_columns, ready, left, cols, acc, old, old_copy.wait, 1.0, scale, out, out_sems)


def cost(columns, units):
    k = sum(b.shape[0] for b in columns)
    wide = columns[0].shape[1]
    return pl.CostEstimate(flops=2 * k * units * wide, bytes_accessed=8 * units * wide + 2 * k * (units + wide), transcendentals=0)


def body(hessian_old, gate_rows, up_rows, gate_columns, up_columns):
    tokens = lax.axis_size("col") * gate_rows.shape[0]
    row, col = lax.axis_index("row"), lax.axis_index("col")
    zl, x = row // 4, row % 4
    zh, y, c = col // 8, (col // 2) % 4, col % 2
    w = way(c)
    cat = lambda *blocks: jnp.concatenate(blocks, axis=0)

    r0 = form_rows(gate_rows, up_rows)
    own = silu_product(gate_columns, up_columns)

    plan = (
        ("za", ("r0",), z_out),
        ("ya1", ("r0",), y_out),
        ("yb1", ("r0",), y_back),
        ("zb", ("r0",), z_back),
        ("xb", ("own",), x_back),
        ("za",),
        ("zf", ("za",), z_out),
        ("ya1",),
        ("yf1", ("ya1",), y_out),
        ("yb1",),
        ("xa", ("own",), x_out),
        ("zb",),
        ("pair", ("own",), z_swap),
        ("xb",),
        ("ya2", ("za", "zb", "zf",), y_out),
        ("zf",),
        ("yb2", ("za", "zb", "zf",), y_back),
        ("yf1",),
        ("xf", ("xa",), x_out),
        ("xa",),
        ("k1", ("ya1", "yb1", "yf1",), core_swap),
        ("pair",),
        ("yf2", ("ya2",), y_out),
        ("ya2",),
        ("xb2", ("pair",), x_back),
        ("yb2",),
        ("xf2", ("xf",), z_swap),
        ("xf",),
        ("k0", ("r0", "za", "zb", "zf",), core_swap),
        ("k1",),
        ("xa2", ("pair",), x_out),
        ("yf2",),
        ("k2", ("ya2", "yb2", "yf2",), core_swap),
        ("k0",),
        ("k2",),
    )
    got = {"r0": r0, "own": own}
    came = {"r0": [(0, 0, 0)], "own": [(0, 0, 0)]}
    for name, *way_there in plan:
        if way_there:
            sources, target = way_there
            move = MOVES[target]
            came[name] = [tuple(p + q for p, q in zip(at, move)) for k in sources for at in came[k]]
    early_names, late_names = ("own", "pair", "xa", "xb", "xf",), ("xa2", "xb2", "xf2",)
    piece_names = ["r0"] + [name for name in came if name[0] in "zyk"]

    def token_block(side, up, other):
        sign = w * (1 - 2 * other)
        return ((zh - sign * up) % 4) * 8 + ((y - sign * side) % 4) * 2 + (c + other) % 2

    def shard(side, up, other):
        return ((zl + up) % 2) * 4 + (x - w * side) % 4

    block_at = [token_block(*at) for name in piece_names for at in came[name]]
    shard_at = [shard(*came[name][0]) for name in early_names + late_names]
    table = jnp.stack(block_at + shard_at).astype(jnp.int32) - 16
    for name, *way_there in plan:
        if way_there:
            sources, target = way_there
            value = got[sources[0]] if len(sources) == 1 else cat(*(got[k] for k in sources))
            table, value = lax.optimization_barrier((table, value))
            got[name] = send(value, target)
        else:
            table, got[name] = lax.optimization_barrier((table + 1, got[name]))

    pieces = [got[name] for name in piece_names]
    early = [got[name] for name in early_names]
    late = [got[name] for name in late_names]
    units, wide = hessian_old.shape
    scale = 1.0 / tokens
    n_blocks = tokens // 128
    n_late = 4 * len(late)
    params = pltpu.CompilerParams(vmem_limit_bytes=58 * 2**20)
    whole = pltpu.VMEM(hessian_old.shape, jnp.float32)
    dma = pltpu.SemaphoreType.DMA
    partial, late_rows = pl.pallas_call(
        functools.partial(early_kernel, len(pieces), len(early), scale),
        out_shape=(jax.ShapeDtypeStruct(hessian_old.shape, jnp.float32), jax.ShapeDtypeStruct((n_late, units, 128), jnp.bfloat16)),
        in_specs=[SMEM, HBM] + [HBM] * (len(pieces) + len(early)),
        out_specs=(HBM, HBM),
        scratch_shapes=[
            pltpu.VMEM((n_blocks, units, 128), jnp.bfloat16),
            pltpu.VMEM((len(early), *own.shape), jnp.bfloat16),
            whole,
            whole,
            dma((n_blocks,)),
            dma((len(early),)),
            dma,
            dma((n_late,)),
            dma((units // CHUNK,)),
        ],
        compiler_params=params,
        cost_estimate=cost(early, units),
    )(table, hessian_old, *pieces, *early)
    partial, *late = lax.optimization_barrier((partial, *late))
    return pl.pallas_call(
        functools.partial(late_kernel, len(late), scale),
        out_shape=jax.ShapeDtypeStruct(hessian_old.shape, jnp.float32),
        in_specs=[HBM] * (2 + len(late)),
        out_specs=HBM,
        scratch_shapes=[
            pltpu.VMEM((n_late, units, 128), jnp.bfloat16),
            pltpu.VMEM((len(late), *own.shape), jnp.bfloat16),
            whole,
            whole,
            dma((len(late),)),
            dma((len(late),)),
            dma,
            dma((units // CHUNK,)),
        ],
        compiler_params=params,
        cost_estimate=cost(late, units),
    )(partial, late_rows, *late)


def solution(mesh):
    in_specs = (P("row", "col"), P("col", "row"), P("col", "row"), P("row", "col"), P("row", "col"))
    out_specs = P("row", "col")
    return jax.shard_map(body, mesh=mesh, in_specs=in_specs, out_specs=out_specs, check_vma=False)
```

```python
import functools

import jax
import jax.numpy as jnp
from jax import lax
from jax.experimental import pallas as pl
from jax.experimental.pallas import tpu as pltpu
from jax.sharding import PartitionSpec as P

AXES = ("row", "col")
CHUNK = 256
VMEM = pl.BlockSpec(memory_space=pltpu.VMEM)
SMEM = pl.BlockSpec(memory_space=pltpu.SMEM)
HBM = pl.BlockSpec(memory_space=pltpu.HBM)


def place(x, y, z, c):
    x, y, z = x % 4, y % 4, z % 8
    return ((z % 2) * 4 + x) * 32 + ((z // 2) * 4 + y) * 2 + c


def send(value, target, after=()):
    if after:
        value = lax.optimization_barrier((value, *after))[0]
    pairs = []
    for x in range(4):
        for y in range(4):
            for z in range(8):
                for c in range(2):
                    pairs.append((place(x, y, z, c), place(*target(x, y, z, c))))
    return lax.ppermute(value, AXES, pairs)


def way(c):
    return 1 - 2 * c


def x_out(x, y, z, c):
    return x + way(c), y, z, c


def x_back(x, y, z, c):
    return x - way(c), y, z, c


def y_out(x, y, z, c):
    return x, y + way(c), z, c


def y_back(x, y, z, c):
    return x, y - way(c), z, c


def z_out(x, y, z, c):
    return x, y, z + 2 * way(c), c


def z_back(x, y, z, c):
    return x, y, z - 2 * way(c), c


def z_swap(x, y, z, c):
    return x, y, z ^ 1, c


def core_swap(x, y, z, c):
    return x, y, z, 1 - c


MOVES = {x_out: (1, 0, 0), x_back: (-1, 0, 0), y_out: (1, 0, 0), y_back: (-1, 0, 0), z_out: (0, 1, 0), z_back: (0, -1, 0), z_swap: (0, 1, 0), core_swap: (0, 0, 1)}


def silu_product(gate, up):
    return (jax.nn.silu(gate.astype(jnp.float32)) * up.astype(jnp.float32)).astype(jnp.bfloat16)


def rows_kernel(gate, up, out):
    gated = gate[...].astype(jnp.float32)
    formed = gated / (1.0 + jnp.exp(-gated)) * up[...].astype(jnp.float32)
    out[0] = formed.T.astype(jnp.bfloat16)


def form_rows(gate, up):
    tokens, units = gate.shape
    return pl.pallas_call(
        rows_kernel,
        out_shape=jax.ShapeDtypeStruct((1, units, tokens), jnp.bfloat16),
        in_specs=[VMEM, VMEM],
        out_specs=VMEM,
        cost_estimate=pl.CostEstimate(flops=8 * gate.size, bytes_accessed=6 * gate.size, transcendentals=gate.size),
    )(gate, up)


def add_up(n, ready, left, cols, acc, first, first_ready, first_scale, scale, out, out_sems):
    units = acc.shape[0]
    done = []
    for index in range(n):
        ready(index)
        for step in range(units // CHUNK):
            part = pl.ds(step * CHUNK, CHUNK)
            product = jnp.dot(left(index, part), cols[index], preferred_element_type=jnp.float32)
            if index == 0:
                acc[part, :] = product
            elif index < n - 1:
                acc[part, :] += product
            else:
                if step == 0:
                    first_ready()
                acc[part, :] = first_scale * first[part, :] + scale * (acc[part, :] + product)
                done.append(pltpu.make_async_copy(acc.at[part], out.at[part], out_sems.at[step]))
                done[-1].start()
    for copy in done:
        copy.wait()


def early_kernel(n_pieces, n_columns, scale, table, hessian, *refs):
    pieces, columns = refs[:n_pieces], refs[n_pieces:n_pieces + n_columns]
    out, late_rows, rows, cols, old, acc, row_sems, col_sems, old_sem, late_sems, out_sems = refs[n_pieces + n_columns:]
    n_blocks = rows.shape[0]
    shard_at = lambda i: table[n_blocks + i]
    col_copies = [pltpu.make_async_copy(block, cols.at[i], col_sems.at[i]) for i, block in enumerate(columns)]
    old_copy = pltpu.make_async_copy(hessian, old, old_sem)
    col_copies[0].start()
    k = 0
    for piece in pieces:
        for i in range(piece.shape[0]):
            at = table[k]
            pltpu.make_async_copy(piece.at[i], rows.at[at], row_sems.at[at]).start()
            k += 1
    for copy in col_copies[1:]:
        copy.start()
    old_copy.start()
    kept = []

    def rows_ready(index):
        for i in range(4):
            at = shard_at(index) * 4 + i
            pltpu.make_async_copy(rows.at[at], rows.at[at], row_sems.at[at]).wait()

    def ready(index):
        rows_ready(index)
        col_copies[index].wait()

    def old_ready():
        old_copy.wait()
        for j in range(late_rows.shape[0] // 4):
            rows_ready(n_columns + j)
            for i in range(4):
                at = shard_at(n_columns + j) * 4 + i
                kept.append(pltpu.make_async_copy(rows.at[at], late_rows.at[j * 4 + i], late_sems.at[j * 4 + i]))
                kept[-1].start()

    def left(index, part):
        at = shard_at(index) * 4
        return jnp.concatenate([rows[at + i, part, :] for i in range(4)], axis=1)

    add_up(n_columns, ready, left, cols, acc, old, old_ready, 0.5, scale, out, out_sems)
    for copy in kept:
        copy.wait()


def late_kernel(n_columns, scale, partial, late_rows, *refs):
    columns = refs[:n_columns]
    out, rows, cols, old, acc, row_sems, col_sems, old_sem, out_sems = refs[n_columns:]
    row_copies, col_copies = [], []
    for i, block in enumerate(columns):
        own = pl.ds(i * 4, 4)
        row_copies.append(pltpu.make_async_copy(late_rows.at[own], rows.at[own], row_sems.at[i]))
        col_copies.append(pltpu.make_async_copy(block, cols.at[i], col_sems.at[i]))
        row_copies[-1].start()
        col_copies[-1].start()
    old_copy = pltpu.make_async_copy(partial, old, old_sem)
    old_copy.start()

    def ready(index):
        row_copies[index].wait()
        col_copies[index].wait()

    def left(index, part):
        return jnp.concatenate([rows[index * 4 + i, part, :] for i in range(4)], axis=1)

    add_up(n_columns, ready, left, cols, acc, old, old_copy.wait, 1.0, scale, out, out_sems)


def cost(columns, units):
    k = sum(b.shape[0] for b in columns)
    wide = columns[0].shape[1]
    return pl.CostEstimate(flops=2 * k * units * wide, bytes_accessed=8 * units * wide + 2 * k * (units + wide), transcendentals=0)


def body(hessian_old, gate_rows, up_rows, gate_columns, up_columns):
    tokens = lax.axis_size("col") * gate_rows.shape[0]
    row, col = lax.axis_index("row"), lax.axis_index("col")
    zl, x = row // 4, row % 4
    zh, y, c = col // 8, (col // 2) % 4, col % 2
    w = way(c)
    cat = lambda *blocks: jnp.concatenate(blocks, axis=0)

    r0 = form_rows(gate_rows, up_rows)
    own = silu_product(gate_columns, up_columns)

    plan = (
        ("za", ("r0",), z_out),
        ("ya1", ("r0",), y_out),
        ("yb1", ("r0",), y_back),
        ("zb", ("r0",), z_back),
        ("xb", ("own",), x_back),
        ("za",),
        ("zf", ("za",), z_out),
        ("ya1",),
        ("yf1", ("ya1",), y_out),
        ("yb1",),
        ("xa", ("own",), x_out),
        ("zb",),
        ("pair", ("own",), z_swap),
        ("xb",),
        ("ya2", ("za", "zb", "zf",), y_out),
        ("zf",),
        ("yb2", ("za", "zb", "zf",), y_back),
        ("yf1",),
        ("xf", ("xa",), x_out),
        ("xa",),
        ("k1", ("ya1", "yb1", "yf1",), core_swap),
        ("pair",),
        ("yf2", ("ya2",), y_out),
        ("ya2",),
        ("xb2", ("pair",), x_back),
        ("yb2",),
        ("xf2", ("xf",), z_swap),
        ("xf",),
        ("k0", ("r0", "za", "zb", "zf",), core_swap),
        ("k1",),
        ("xa2", ("pair",), x_out),
        ("yf2",),
        ("k2", ("ya2", "yb2", "yf2",), core_swap),
        ("k0",),
        ("k2",),
    )
    got = {"r0": r0, "own": own}
    came = {"r0": [(0, 0, 0)], "own": [(0, 0, 0)]}
    for name, *way_there in plan:
        if way_there:
            sources, target = way_there
            move = MOVES[target]
            came[name] = [tuple(p + q for p, q in zip(at, move)) for k in sources for at in came[k]]
    early_names, late_names = ("own", "pair", "xa", "xb", "xf",), ("xa2", "xb2", "xf2",)
    piece_names = ["r0"] + [name for name in came if name[0] in "zyk"]

    def token_block(side, up, other):
        sign = w * (1 - 2 * other)
        return ((zh - sign * up) % 4) * 8 + ((y - sign * side) % 4) * 2 + (c + other) % 2

    def shard(side, up, other):
        return ((zl + up) % 2) * 4 + (x - w * side) % 4

    block_at = [token_block(*at) for name in piece_names for at in came[name]]
    shard_at = [shard(*came[name][0]) for name in early_names + late_names]
    table = jnp.stack(block_at + shard_at).astype(jnp.int32) - 16
    for name, *way_there in plan:
        if way_there:
            sources, target = way_there
            value = got[sources[0]] if len(sources) == 1 else cat(*(got[k] for k in sources))
            table, value = lax.optimization_barrier((table, value))
            got[name] = send(value, target)
        else:
            table, got[name] = lax.optimization_barrier((table + 1, got[name]))

    pieces = [got[name] for name in piece_names]
    early = [got[name] for name in early_names]
    late = [got[name] for name in late_names]
    units, wide = hessian_old.shape
    scale = 1.0 / tokens
    n_blocks = tokens // 128
    n_late = 4 * len(late)
    params = pltpu.CompilerParams(vmem_limit_bytes=58 * 2**20)
    whole = pltpu.VMEM(hessian_old.shape, jnp.float32)
    dma = pltpu.SemaphoreType.DMA
    partial, late_rows = pl.pallas_call(
        functools.partial(early_kernel, len(pieces), len(early), scale),
        out_shape=(jax.ShapeDtypeStruct(hessian_old.shape, jnp.float32), jax.ShapeDtypeStruct((n_late, units, 128), jnp.bfloat16)),
        in_specs=[SMEM, HBM] + [HBM] * (len(pieces) + len(early)),
        out_specs=(HBM, HBM),
        scratch_shapes=[
            pltpu.VMEM((n_blocks, units, 128), jnp.bfloat16),
            pltpu.VMEM((len(early), *own.shape), jnp.bfloat16),
            whole,
            whole,
            dma((n_blocks,)),
            dma((len(early),)),
            dma,
            dma((n_late,)),
            dma((units // CHUNK,)),
        ],
        compiler_params=params,
        cost_estimate=cost(early, units),
    )(table, hessian_old, *pieces, *early)
    partial, *late = lax.optimization_barrier((partial, *late))
    return pl.pallas_call(
        functools.partial(late_kernel, len(late), scale),
        out_shape=jax.ShapeDtypeStruct(hessian_old.shape, jnp.float32),
        in_specs=[HBM] * (2 + len(late)),
        out_specs=HBM,
        scratch_shapes=[
            pltpu.VMEM((n_late, units, 128), jnp.bfloat16),
            pltpu.VMEM((len(late), *own.shape), jnp.bfloat16),
            whole,
            whole,
            dma((len(late),)),
            dma((len(late),)),
            dma,
            dma((units // CHUNK,)),
        ],
        compiler_params=params,
        cost_estimate=cost(late, units),
    )(partial, late_rows, *late)


def solution(mesh):
    in_specs = (P("row", "col"), P("col", "row"), P("col", "row"), P("row", "col"), P("row", "col"))
    out_specs = P("row", "col")
    return jax.shard_map(body, mesh=mesh, in_specs=in_specs, out_specs=out_specs, check_vma=False)
```
